32 devices in a mesh: lat: 4 (over x, core), lon: 8 (over z, y).
Axes of the slice: x: 2, y: 2, z: 4, core: 2. Of those that a mesh axis runs over, the one named last changes fastest.
Arguments:
- fields: float32 [4, 90, 64, 1024], P(None, None, 'lat', 'lon'), may hold values from -6 to 6
- courant_lon: float32 [90, 64, 1024], P(None, 'lat', 'lon'), may hold values from -0.3 to 0.3
- courant_lat: float32 [90, 64, 1024], P(None, 'lat', 'lon'), may hold values from -0.3 to 0.3
- diffusion: float32 [90, 64, 1024], P(None, 'lat', 'lon'), may hold values from 0.1 to 0.24
- tend_cot: bfloat16 [4, 90, 64, 1024], P(None, None, 'lat', 'lon'), may hold values from -6 to 6
- col_list: int32 [4, 8, 1024], P('lat', 'lon'), may hold values from 0 to 2047, as said below
- block_count: int32 [4, 8, 8], P('lat', 'lon'), may hold values from 1 to 128, as said below
- block_dest: int32 [4, 8, 8], P('lat', 'lon'), may hold values from 0 to 7, each once within a row
- w_in: bfloat16 [8, 360, 512], P('lon', None, 'lat'), may hold values from -0.3125 to 0.3125
- w_mid: bfloat16 [8, 512, 512], P('lon', None, 'lat'), may hold values from -0.25 to 0.25
- w_out: bfloat16 [8, 360, 512], P('lon', None, 'lat'), may hold values from -0.25 to 0.25
Outputs:
- new_fields: float32 [4, 90, 64, 1024], P(None, None, 'lat', 'lon')
- adjoint: bfloat16 [4, 90, 64, 1024], P(None, None, 'lat', 'lon')
- grad_in: float32 [8, 360, 512], P('lon', None, 'lat')
- grad_mid: float32 [8, 512, 512], P('lon', None, 'lat')
- grad_out: float32 [8, 360, 512], P('lon', None, 'lat')
The draws below stay inside these ranges and needn't reach their ends.
Inputs may be any that keep to these rules, and one draw needn't show every extreme that they name: `col_list`: within one tile's list no local column appears twice. `block_count`: in each tile one block has all 128 slots live. `block_dest`: each tile's row names every expert exactly once.
All inputs are finite; a program needn't handle non-finite values.
Results may differ from the reference program's by a relative error of at most 0.0074.
Values may be sent and summed in bfloat16 or wider, within the bound.
A program may use at most 320 MiB of HBM per device.

```python
import jax
import jax.numpy as jnp
from jax import lax

LEV = 90
FEAT = 360
HID = 512
CLAT = 16
CLON = 128
BLK = 128
STEPS = 4
NLAT = 64
NLON = 1024
EXPERTS = 8
N_LAT = 4
N_LON = 8


def draw_col_list(key, part):
    keys = jax.random.split(jax.random.fold_in(key, 11), N_LAT * N_LON)

    def one(single):
        return jax.random.permutation(single, CLAT * CLON)[:BLK * N_LON].astype(jnp.int32)
    return jax.vmap(one)(keys).reshape(N_LAT, N_LON, BLK * N_LON)


def draw_block_count(key, part):
    base = jax.random.fold_in(key, 23)
    key_level, key_raw, key_full = jax.random.split(base, 3)
    level = jax.random.randint(key_level, (N_LAT, N_LON, 1), 0, 4)
    raw = jax.random.randint(key_raw, (N_LAT, N_LON, N_LON), 0, 3 * BLK // 4) + level * (BLK // 4) + 1
    full = jax.random.randint(key_full, (N_LAT, N_LON, 1), 0, N_LON)
    index = jnp.arange(N_LON, dtype=jnp.int32)[None, None, :]
    return jnp.where(index == full, BLK, jnp.minimum(raw, BLK)).astype(jnp.int32)


def steps_of(key, extent, pieces, low, high):
    gain, own = 1.0, jax.random.fold_in(key, 6)
    for dim, shards_of in pieces:
        steps = jnp.exp(jax.random.uniform(jax.random.fold_in(own, dim), (shards_of,), jnp.float32, low / len(pieces), high / len(pieces)))
        gain = gain * jnp.repeat(steps, extent[dim] // shards_of).reshape([-1 if axis == dim else 1 for axis in range(len(extent))])
    return gain


def noise(own_key, dims, deviation, reach, cuts=(), held_as=jnp.bfloat16):
    loudness = steps_of(own_key, dims, cuts, -0.22, 0.18) if cuts else 1.0
    entries = jax.random.normal(own_key, dims, jnp.float32) * deviation * loudness
    return jnp.minimum(jnp.maximum(entries, -reach), reach).astype(held_as)


def setup_inputs(seed: int = 0) -> dict:
    streams_of = jax.random.split(jax.random.key(seed), 12)
    return {
        "fields": noise(streams_of[0], (4, LEV, NLAT, NLON), 1.0, 6.0, ((2, 4), (3, 8)), jnp.float32),
        "courant_lon": jnp.clip(jax.random.uniform(streams_of[1], (LEV, NLAT, NLON), jnp.float32, -0.3, 0.3) * steps_of(streams_of[1], (LEV, NLAT, NLON), ((1, 4), (2, 8)), -0.4, 0.0), -0.3, 0.3),
        "courant_lat": jnp.clip(jax.random.uniform(streams_of[2], (LEV, NLAT, NLON), jnp.float32, -0.3, 0.3) * steps_of(streams_of[2], (LEV, NLAT, NLON), ((1, 4), (2, 8)), -0.4, 0.0), -0.3, 0.3),
        "diffusion": jnp.clip(0.1 + 0.13999999 * jax.random.uniform(streams_of[3], (LEV, NLAT, NLON), jnp.float32) ** steps_of(streams_of[3], (LEV, NLAT, NLON), ((1, 4), (2, 8)), -0.2, 0.2), 0.1, 0.24),
        "tend_cot": noise(streams_of[4], (4, LEV, NLAT, NLON), 1.0, 6.0, ((2, 4), (3, 8))),
        "col_list": draw_col_list(jax.random.fold_in(streams_of[11], 71), 0),
        "block_count": draw_block_count(jax.random.fold_in(streams_of[11], 71), 0),
        "block_dest": jax.vmap(lambda own: jax.random.permutation(own, N_LON))(jax.random.split(streams_of[7], N_LAT * N_LON)).reshape((N_LAT, N_LON, N_LON)).astype(jnp.int32),
        "w_in": noise(streams_of[8], (EXPERTS, FEAT, HID), FEAT ** -0.5, 0.3125, ((0, 8), (2, 4))),
        "w_mid": noise(streams_of[9], (EXPERTS, HID, HID), HID ** -0.5, 0.25, ((0, 8), (2, 4))),
        "w_out": noise(streams_of[10], (EXPERTS, FEAT, HID), HID ** -0.5, 0.25, ((0, 8), (2, 4))),
    }


def dsilu(value):
    sig = jax.nn.sigmoid(value)
    return sig * (1.0 + value * (1.0 - sig))

def physics(x, g, weights, shared):
    w_first, w_second, w_third = weights
    lead = 'e' if shared else 'b'
    xf = x.astype(jnp.float32)
    scale = lax.rsqrt(lax.optimization_barrier(jnp.mean(xf * xf, axis=0, keepdims=True)) + 1e-06)
    xn = (xf * scale).astype(jnp.bfloat16)
    a_one = jnp.einsum(lead + 'fh,fbc->hbc', w_first, xn, preferred_element_type=jnp.float32)
    h_one = jax.nn.silu(a_one).astype(jnp.bfloat16)
    a_two = jnp.einsum(lead + 'gh,gbc->hbc', w_second, h_one, preferred_element_type=jnp.float32)
    h_two = jax.nn.silu(a_two).astype(jnp.bfloat16)
    tend = jnp.einsum(lead + 'fh,hbc->fbc', w_third, h_two, preferred_element_type=jnp.float32).astype(jnp.bfloat16)
    back_two = jnp.einsum(lead + 'fh,fbc->hbc', w_third, g, preferred_element_type=jnp.float32)
    d_two = (back_two * dsilu(a_two)).astype(jnp.bfloat16)
    back_one = jnp.einsum(lead + 'gh,hbc->gbc', w_second, d_two, preferred_element_type=jnp.float32)
    d_one = (back_one * dsilu(a_one)).astype(jnp.bfloat16)
    d_norm = jnp.einsum(lead + 'fh,hbc->fbc', w_first, d_one, preferred_element_type=jnp.float32)
    adj = (scale * d_norm - xf * (scale * scale * scale) * lax.optimization_barrier(jnp.mean(xf * d_norm, axis=0, keepdims=True))).astype(jnp.bfloat16)
    out_form = 'fh' if shared else 'bfh'
    mid_form = 'gh' if shared else 'bgh'
    grad_first = jnp.einsum('fbc,hbc->' + out_form, xn, d_one, preferred_element_type=jnp.float32)
    grad_second = jnp.einsum('gbc,hbc->' + mid_form, h_one, d_two, preferred_element_type=jnp.float32)
    grad_third = jnp.einsum('fbc,hbc->' + out_form, g, h_two, preferred_element_type=jnp.float32)
    return (tend, adj, (grad_first, grad_second, grad_third))

def reference(fields, courant_lon, courant_lat, diffusion, tend_cot, col_list, block_count, block_dest, w_in, w_mid, w_out):
    state = fields
    for step in range(STEPS):
        east = jnp.roll(state, -1, axis=3)
        west = jnp.roll(state, 1, axis=3)
        padded = jnp.pad(state, ((0, 0), (0, 0), (1, 1), (0, 0)))
        north = padded[:, :, 2:]
        south = padded[:, :, :-2]
        state = state - 0.5 * courant_lon * (east - west) - 0.5 * courant_lat * (north - south) + diffusion * (east + west + north + south - 4.0 * state)
    feat = 4 * LEV
    ncol = CLAT * CLON
    devs = N_LAT * N_LON

    def tiles(array):
        return array.reshape(4, LEV, N_LAT, CLAT, N_LON, CLON).transpose(2, 4, 0, 1, 3, 5).reshape(N_LAT, N_LON, feat, ncol)

    def untile(array):
        return array.reshape(N_LAT, N_LON, 4, LEV, CLAT, CLON).transpose(2, 3, 0, 4, 1, 5).reshape(4, LEV, N_LAT * CLAT, N_LON * CLON)
    col_tiles = tiles(fields.astype(jnp.bfloat16))
    cot_tiles = tiles(tend_cot)
    slot_table = col_list.reshape(N_LAT, N_LON, N_LON, BLK)

    def expert(index):
        pick = (block_dest == index).astype(jnp.int32)
        which = jnp.argmax(pick, axis=2).astype(jnp.int32)
        cols = jnp.take_along_axis(slot_table, which[:, :, None, None], axis=2)[:, :, 0]
        count = jnp.take_along_axis(block_count, which[:, :, None], axis=2)[:, :, 0]
        live = jnp.arange(BLK, dtype=jnp.int32)[None, None, :] < count[:, :, None]
        xs = jnp.take_along_axis(col_tiles, cols[:, :, None, :], axis=3)
        gs = jnp.take_along_axis(cot_tiles, cols[:, :, None, :], axis=3)
        xs = jnp.where(live[:, :, None, :], xs, jnp.zeros_like(xs))
        gs = jnp.where(live[:, :, None, :], gs, jnp.zeros_like(gs))
        x_block = xs.reshape(devs, feat, BLK).transpose(1, 0, 2)
        g_block = gs.reshape(devs, feat, BLK).transpose(1, 0, 2)
        weights = (w_in[index][None], w_mid[index][None], w_out[index][None])
        tend, adj, grads = physics(x_block, g_block, weights, True)
        return (tend, adj, cols.reshape(devs, BLK), grads[0], grads[1], grads[2])
    tends, adjs, cols_all, grad_in, grad_mid, grad_out = lax.map(expert, jnp.arange(N_LON, dtype=jnp.int32))
    dev_index = jnp.broadcast_to(jnp.arange(devs, dtype=jnp.int32)[None, :, None], cols_all.shape)
    tend_full = jnp.zeros((devs, feat, ncol), jnp.bfloat16).at[dev_index, :, cols_all].set(tends.transpose(0, 2, 3, 1))
    adj_full = jnp.zeros((devs, feat, ncol), jnp.bfloat16).at[dev_index, :, cols_all].set(adjs.transpose(0, 2, 3, 1))
    new_fields = state + untile(tend_full).astype(jnp.float32)
    adjoint = untile(adj_full)
    return (new_fields, adjoint, grad_in, grad_mid, grad_out)
```

```python
import jax
import jax.numpy as jnp
from jax import lax
from jax.experimental import pallas as pl
from jax.experimental.pallas import tpu as pltpu
from jax.sharding import PartitionSpec as P

STEPS = 4
F32 = jnp.float32
BF16 = jnp.bfloat16
MESH = pl.DeviceIdType.MESH


def mm(a, b):
    return jnp.dot(a, b, preferred_element_type=F32)


def mm_nt(a, b):
    return lax.dot_general(a, b, (((1,), (1,)), ((), ())), preferred_element_type=F32)


def mm_tn(a, b):
    return lax.dot_general(a, b, (((0,), (0,)), ((), ())), preferred_element_type=F32)


def sigmoid(v):
    return 1.0 / (1.0 + jnp.exp(-v))


def make_kernel(nlat, nlon, nfield, levels, rows, width, hid):
    feat = nfield * levels
    ncol = rows * width
    hl = hid // nlat
    npair = nlon // 2
    nk = nlon * 128

    def kernel(
        fields, clon, clat, cdif, cot, cols, wi_t, wm_t, wo_t,
        out_f, out_a, out_gi, out_gm, out_go,
        wide, data, hot, xs, xr, ts, tr,
        wi, wm, wo, hx, hg, h1s, h2s, d1s, d2s, gs, gr,
        rim_rows, rim_lanes, got_rows, got_lanes,
        send_rows, send_lanes, recv_rows, recv_lanes,
        w_send, w_recv, x_send, x_recv, t_send, t_recv, g_send, g_recv, r_send, r_recv,
    ):
        lat = lax.axis_index("lat")
        lon = lax.axis_index("lon")
        pair_me = lon // 2

        barrier = pltpu.get_barrier_semaphore()
        for off in range(1, nlon):
            pl.semaphore_signal(
                barrier, inc=1, device_id=(lat, lax.rem(lon + off, nlon)), device_id_type=MESH
            )
        for off in range(1, nlat):
            pl.semaphore_signal(
                barrier, inc=1, device_id=(lax.rem(lat + off, nlat), lon), device_id_type=MESH
            )
        pl.semaphore_wait(barrier, nlon + nlat - 2)

        def rim_copy(step, way):
            target = (
                (lat, lax.rem(lon + nlon - 1, nlon)),
                (lat, lax.rem(lon + 1, nlon)),
                (lax.rem(lat + nlat - 1, nlat), lon),
                (lax.rem(lat + 1, nlat), lon),
            )[way]
            source, place = (
                (send_lanes, recv_lanes) if way < 2 else (send_rows, recv_rows)
            )
            return pltpu.make_async_remote_copy(
                src_ref=source.at[step, way % 2],
                dst_ref=place.at[step, way % 2],
                send_sem=r_send.at[step, way],
                recv_sem=r_recv.at[step, way],
                device_id=target,
                device_id_type=MESH,
            )

        lane = lax.broadcasted_iota(jnp.int32, (rows, width), 1)
        row = lax.broadcasted_iota(jnp.int32, (rows, width), 0)

        def keep_rims(value, c, level):
            f = c * levels + level
            here = pl.ds(c * rows, rows)
            rim_lanes[0, here, :] = jnp.where(
                lane == level, jnp.broadcast_to(value[:, :1], value.shape), rim_lanes[0, here, :]
            )
            rim_lanes[1, here, :] = jnp.where(
                lane == level + 1,
                jnp.broadcast_to(value[:, width - 1 :], value.shape),
                rim_lanes[1, here, :],
            )
            rim_rows[0, pl.ds(f, 1), :] = value[:1, :]
            rim_rows[1, pl.ds(f, 1), :] = value[rows - 1 :, :]

        def send_rims(step):
            send_lanes[step] = rim_lanes[...].astype(BF16)
            send_rows[step] = rim_rows[...].astype(BF16)
            for way in range(4):
                rim_copy(step, way).start()

        rim_lanes[...] = jnp.zeros_like(rim_lanes)
        rim_rows[...] = jnp.zeros_like(rim_rows)

        @pl.loop(0, levels)
        def _(level):
            for c in range(nfield):
                keep_rims(
                    fields[pl.ds(pl.multiple_of((c * levels + level) * rows, rows), rows), :],
                    c,
                    level,
                )

        send_rims(0)

        full_w = (wi, wm, wo)
        own_w = (wi_t, wm_t, wo_t)
        place_w = pl.ds(pl.multiple_of(lat * hl, hl), hl)

        def weight_copy(which, off):
            other = lax.rem(lat + off, nlat)
            return pltpu.make_async_remote_copy(
                src_ref=own_w[which],
                dst_ref=full_w[which].at[place_w, :],
                send_sem=w_send.at[which, off],
                recv_sem=w_recv.at[which, off],
                device_id=(other, lon),
                device_id_type=MESH,
            )

        for which in range(3):
            for off in range(1, nlat):
                weight_copy(which, off).start()
            full_w[which][place_w, :] = own_w[which][...]

        wide[...] = cot[...].astype(F32)
        for r in range(rows):
            part = jnp.concatenate(
                [
                    fields[pl.ds(r, feat, stride=rows), :],
                    wide[pl.ds(r, feat, stride=rows), :],
                ],
                axis=0,
            )
            data[:, r * width : (r + 1) * width] = part.astype(BF16)

        def block_copy(source, place, sends, recvs, other):
            return pltpu.make_async_remote_copy(
                src_ref=source.at[other],
                dst_ref=place.at[lon],
                send_sem=sends.at[other],
                recv_sem=recvs.at[lon],
                device_id=(lat, other),
                device_id_type=MESH,
            )

        def block_wait(source, place, sends, recvs, other):
            return pltpu.make_async_remote_copy(
                src_ref=source.at[other],
                dst_ref=place.at[other],
                send_sem=sends.at[other],
                recv_sem=recvs.at[other],
                device_id=(lat, other),
                device_id_type=MESH,
            )

        def ship(source, place, sends, recvs, other):
            @pl.when(other != lon)
            def _():
                block_copy(source, place, sends, recvs, other).start()

            @pl.when(other == lon)
            def _():
                place[lon] = source[lon]

        def arrive(source, place, sends, recvs, other):
            @pl.when(other != lon)
            def _():
                block_wait(source, place, sends, recvs, other).wait_recv()

        @pl.loop(0, npair)
        def _(i):
            p = lax.rem(pair_me + 1 + i, npair)
            at = pl.ds(pl.multiple_of(p * 256, 256), 256)
            names = cols[:, at]
            index = lax.broadcasted_iota(jnp.int32, (ncol, 256), 0)
            hot[:, at] = jnp.where(index == names, 1.0, 0.0).astype(BF16)
            picked = mm(data[...], hot[:, at]).astype(BF16)
            for half in range(2):
                xs[2 * p + half] = picked[:, half * 128 : (half + 1) * 128]
                ship(xs, xr, x_send, x_recv, 2 * p + half)

        top = (lat < nlat - 1).astype(F32)
        bottom = (lat > 0).astype(F32)

        def dynamics(step):
            for way in range(4):
                rim_copy(step, way).wait_recv()
            got_lanes[...] = recv_lanes[step].astype(F32)
            got_rows[0] = recv_rows[step, 0].astype(F32) * top
            got_rows[1] = recv_rows[step, 1].astype(F32) * bottom
            origin = fields if step == 0 else out_f

            @pl.loop(0, levels)
            def _(level):
                flat = pl.ds(pl.multiple_of(level * rows, rows), rows)
                half_lon = 0.5 * clon[flat, :]
                half_lat = 0.5 * clat[flat, :]
                dif = cdif[flat, :]
                c_here = 1.0 - 4.0 * dif
                c_east, c_west = dif - half_lon, dif + half_lon
                c_north, c_south = dif - half_lat, dif + half_lat
                for c in range(nfield):
                    f = c * levels + level
                    at = pl.ds(pl.multiple_of(f * rows, rows), rows)
                    here = pl.ds(c * rows, rows)
                    v = origin[at, :]
                    shift = width - 1 - level
                    east = jnp.where(
                        lane == width - 1,
                        pltpu.roll(got_lanes[0, here, :], shift, 1),
                        pltpu.roll(v, width - 1, 1),
                    )
                    west = jnp.where(
                        lane == 0,
                        pltpu.roll(got_lanes[1, here, :], shift, 1),
                        pltpu.roll(v, 1, 1),
                    )
                    north = jnp.where(
                        row == rows - 1,
                        jnp.broadcast_to(got_rows[0, pl.ds(f, 1), :], v.shape),
                        pltpu.roll(v, rows - 1, 0),
                    )
                    south = jnp.where(
                        row == 0,
                        jnp.broadcast_to(got_rows[1, pl.ds(f, 1), :], v.shape),
                        pltpu.roll(v, 1, 0),
                    )
                    new = (
                        c_here * v + c_east * east + c_west * west + c_north * north + c_south * south
                    )
                    out_f[at, :] = new
                    if step < STEPS - 1:
                        keep_rims(new, c, level)

            if step < STEPS - 1:
                send_rims(step + 1)

        dynamics(0)
        dynamics(1)
        dynamics(2)

        for which in range(3):
            for off in range(1, nlat):
                weight_copy(which, off).wait_recv()

        @pl.loop(0, npair)
        def _(i):
            p = lax.rem(pair_me + npair - i, npair)
            at = pl.ds(pl.multiple_of(p * 256, 256), 256)
            for half in range(2):
                arrive(xs, xr, x_send, x_recv, 2 * p + half)
            both = jnp.concatenate([xr[2 * p], xr[2 * p + 1]], axis=1).astype(F32)
            x = both[:feat]
            g = both[feat:].astype(BF16)
            scale = lax.rsqrt(jnp.mean(x * x, axis=0, keepdims=True) + 1e-06)
            xn = (x * scale).astype(BF16)
            hx[:, at] = xn
            hg[:, at] = g
            a1 = mm(wi[...], xn)
            s1 = sigmoid(a1)
            h1 = (a1 * s1).astype(BF16)
            h1s[:, at] = h1
            a2 = mm(wm[...], h1)
            s2 = sigmoid(a2)
            h2 = (a2 * s2).astype(BF16)
            h2s[:, at] = h2
            tend = mm_tn(wo[...], h2)
            d2 = (mm(wo[...], g) * (s2 * (1.0 + a2 * (1.0 - s2)))).astype(BF16)
            d2s[:, at] = d2
            d1 = (mm_tn(wm[...], d2) * (s1 * (1.0 + a1 * (1.0 - s1)))).astype(BF16)
            d1s[:, at] = d1
            dxn = mm_tn(wi[...], d1)
            adj = scale * dxn - x * (scale * scale * scale) * jnp.mean(x * dxn, axis=0, keepdims=True)
            back = jnp.concatenate([tend, adj], axis=0).astype(BF16)
            for half in range(2):
                ts[2 * p + half] = back[:, half * 128 : (half + 1) * 128]
                ship(ts, tr, t_send, t_recv, 2 * p + half)

        def partial(owner):
            at = pl.ds(pl.multiple_of(owner * hl, hl), hl)
            return (
                mm_nt(hx[...], d1s[at, :]),
                mm_nt(h1s[...], d2s[at, :]),
                mm_nt(hg[...], h2s[at, :]),
            )

        def grad_copy(off):
            other = lax.rem(lat + off, nlat)
            return pltpu.make_async_remote_copy(
                src_ref=gs.at[off],
                dst_ref=gr.at[off],
                send_sem=g_send.at[off],
                recv_sem=g_recv.at[off],
                device_id=(other, lon),
                device_id_type=MESH,
            )

        @pl.loop(1, nlat)
        def _(off):
            gs[off] = jnp.concatenate(partial(lax.rem(lat + off, nlat)), axis=0).astype(BF16)
            grad_copy(off).start()

        out_gi[...], out_gm[...], out_go[...] = partial(lat)

        dynamics(3)

        @pl.loop(0, nlon)
        def _(e):
            arrive(ts, tr, t_send, t_recv, e)
            data[:, pl.ds(pl.multiple_of(e * 128, 128), 128)] = tr[e]

        for q in range(rows // 2):
            spread = mm_nt(data[:, :nk], hot[q * 256 : (q + 1) * 256, :])
            for half in range(2):
                at = pl.ds(2 * q + half, feat, stride=rows)
                block = spread[:, half * 128 : (half + 1) * 128]
                out_f[at, :] = out_f[at, :] + block[:feat]
                wide[at, :] = block[feat:]
        out_a[...] = wide[...].astype(BF16)

        @pl.loop(1, nlat)
        def _(off):
            grad_copy(off).wait_recv()
            total = gr[off].astype(F32)
            out_gi[...] += total[:feat]
            out_gm[...] += total[feat : feat + hid]
            out_go[...] += total[feat + hid :]

        for step in range(STEPS):
            for way in range(4):
                rim_copy(step, way).wait_send()
        for which in range(3):
            for off in range(1, nlat):
                weight_copy(which, off).wait_send()
        for off in range(1, nlat):
            grad_copy(off).wait_send()

        @pl.loop(0, nlon)
        def _(e):
            @pl.when(e != lon)
            def _():
                block_copy(xs, xr, x_send, x_recv, e).wait_send()
                block_copy(ts, tr, t_send, t_recv, e).wait_send()

    def vm(*shape, dtype=BF16):
        return pltpu.VMEM(shape, dtype)

    frows = (feat + 15) // 16 * 16
    dma = pltpu.SemaphoreType.DMA
    scratch = [
        vm(feat * rows, width, dtype=F32),
        vm(2 * feat, ncol),
        vm(ncol, nk),
        vm(nlon, 2 * feat, 128), vm(nlon, 2 * feat, 128),
        vm(nlon, 2 * feat, 128), vm(nlon, 2 * feat, 128),
        vm(hid, feat), vm(hid, hid), vm(hid, feat),
        vm(feat, nk), vm(feat, nk),
        vm(hid, nk), vm(hid, nk), vm(hid, nk), vm(hid, nk),
        vm(nlat, 2 * feat + hid, hl), vm(nlat, 2 * feat + hid, hl),
        vm(2, frows, width, dtype=F32), vm(2, nfield * rows, width, dtype=F32),
        vm(2, frows, width, dtype=F32), vm(2, nfield * rows, width, dtype=F32),
        vm(STEPS, 2, frows, width), vm(STEPS, 2, nfield * rows, width),
        vm(STEPS, 2, frows, width), vm(STEPS, 2, nfield * rows, width),
        dma((3, nlat)), dma((3, nlat)),
        dma((nlon,)), dma((nlon,)), dma((nlon,)), dma((nlon,)),
        dma((nlat,)), dma((nlat,)),
        dma((STEPS, 4)), dma((STEPS, 4)),
    ]
    outs = [
        jax.ShapeDtypeStruct((feat * rows, width), F32),
        jax.ShapeDtypeStruct((feat * rows, width), BF16),
        jax.ShapeDtypeStruct((feat, hl), F32),
        jax.ShapeDtypeStruct((hid, hl), F32),
        jax.ShapeDtypeStruct((feat, hl), F32),
    ]
    return pl.pallas_call(
        kernel,
        out_shape=outs,
        in_specs=[pl.BlockSpec(memory_space=pltpu.VMEM)] * 9,
        out_specs=[pl.BlockSpec(memory_space=pltpu.VMEM)] * 5,
        scratch_shapes=scratch,
        compiler_params=pltpu.CompilerParams(
            collective_id=0, has_side_effects=True, vmem_limit_bytes=62 * 2**20
        ),
        name="window",
    )


def shards(
    fields, courant_lon, courant_lat, diffusion, tend_cot,
    col_list, block_count, block_dest, w_in, w_mid, w_out,
):
    nfield, levels, rows, width = fields.shape
    nlat, nlon = lax.axis_size("lat"), lax.axis_size("lon")
    hid = w_mid.shape[1]
    nblock = block_dest.shape[-1]
    block_len = col_list.shape[-1] // nblock
    dest = block_dest.reshape(nblock)
    counts = block_count.reshape(nblock)
    slot = jnp.arange(block_len, dtype=jnp.int32)
    named = jnp.where(
        slot[None, :] < counts[:, None], col_list.reshape(nblock, block_len), rows * width
    )
    mine = dest[None, :] == jnp.arange(nblock, dtype=jnp.int32)[:, None]
    cols = jnp.sum(jnp.where(mine[:, :, None], named[None], 0), axis=1).reshape(1, -1)
    flat = lambda a: a.reshape(-1, width)
    new, adj, gi, gm, go = make_kernel(nlat, nlon, nfield, levels, rows, width, hid)(
        flat(fields), flat(courant_lon), flat(courant_lat), flat(diffusion), flat(tend_cot),
        cols, w_in[0].T, w_mid[0].T, w_out[0].T,
    )
    return (new.reshape(fields.shape), adj.reshape(fields.shape), gi[None], gm[None], go[None])


def solution(mesh):
    tile = P(None, None, "lat", "lon")
    plane = P(None, "lat", "lon")
    table = P("lat", "lon", None)
    weight = P("lon", None, "lat")
    return jax.shard_map(
        shards,
        mesh=mesh,
        in_specs=(tile, plane, plane, plane, tile, table, table, table, weight, weight, weight),
        out_specs=(tile, tile, weight, weight, weight),
        check_vma=False,
    )
```
